128 devices in a mesh: cfg: 2 (over z_hi), tm: 8 (over z_lo, x), height: 8 (over y, core).
Axes of the slice: x: 4, y: 4, z: 4 (z_hi: 2, z_lo: 2; z = z_hi * 2 + z_lo), core: 2. Of those that a mesh axis runs over, the one named last changes fastest.
Arguments:
- query: bfloat16 [2, 8, 8, 1, 384, 1536], P('cfg', 'tm', 'height'), may hold values from -6.5 to 6.5
- keyval: bfloat16 [2, 2, 8, 8, 1, 384, 1536], P(None, 'cfg', 'tm', 'height'), may hold values from -6.5 to 6.5
- hidden: bfloat16 [2, 8, 8, 1, 384, 3072], P('cfg', 'tm', 'height'), may hold values from -3 to 3
- out_weight: bfloat16 [1536, 3072], replicated, may hold values from -0.15625 to 0.15625
- gate_scale: float32 [2, 3072], P('cfg'), may hold values from 0.5 to 2
- guidance: float32 [1], replicated, may hold values from 1.5 to 4
- counts: int32 [8, 8, 1], replicated, may hold values from 192 to 384, as said below
Outputs:
- guided: bfloat16 [8, 8, 1, 384, 3072], P('tm', 'height', None, None, 'cfg')
The draws below stay inside these ranges and needn't reach their ends.
Inputs may be any that keep to these rules, and one draw needn't show every extreme that they name: `counts`: A tile's valid tokens are its first ones; every tile outside the last time tile and the last height tile has 384.
All inputs are finite; a program needn't handle non-finite values.
Results may differ from the reference program's by a relative error of at most 0.011.
Values may be sent and summed in bfloat16 or wider, within the bound.
A program may use at most 192 MiB of HBM per device.

```python
import math
import jax
import jax.numpy as jnp
from jax import lax

D = 3072
HEADS = 12
HEAD_DIM = 128
TILE = 384
WIDTH_TILES = 1
CHANNELS = 1536
TIME_TILES = 8
HEIGHT_TILES = 8


def draw_query(key, part):
    shape = (2, TIME_TILES, HEIGHT_TILES, WIDTH_TILES, TILE, CHANNELS)
    base = 1.6 * jax.random.truncated_normal(jax.random.fold_in(key, 1), -4.0, 4.0, shape, jnp.float32)
    return base.astype(jnp.bfloat16)


def draw_keyval(key, part):
    shape = (2, 2, TIME_TILES, HEIGHT_TILES, WIDTH_TILES, TILE, CHANNELS)
    base = 1.6 * jax.random.truncated_normal(jax.random.fold_in(key, 2), -4.0, 4.0, shape, jnp.float32)
    return base.astype(jnp.bfloat16)


def draw_counts(key, part):
    shape = (TIME_TILES, HEIGHT_TILES, WIDTH_TILES)
    ragged_values = jax.random.randint(jax.random.fold_in(key, 4), shape, TILE // 2, TILE + 1, jnp.int32)
    time_at = jnp.arange(TIME_TILES, dtype=jnp.int32).reshape(TIME_TILES, 1, 1)
    height_at = jnp.arange(HEIGHT_TILES, dtype=jnp.int32).reshape(1, HEIGHT_TILES, 1)
    ragged = (time_at == TIME_TILES - 1) | (height_at == HEIGHT_TILES - 1)
    return jnp.where(ragged, ragged_values, TILE).astype(jnp.int32)


def block_scale(own_key, shape, cuts, smallest, largest):
    def one(dim, parts):
        steps = jax.random.uniform(jax.random.fold_in(jax.random.fold_in(own_key, 6), dim), (parts,), jnp.float32, smallest / len(cuts), largest / len(cuts))
        return jnp.repeat(jnp.exp(steps), shape[dim] // parts).reshape((-1,) + (1,) * (len(shape) - dim - 1))

    factor_of = one(*cuts[0])
    for cut in cuts[1:]:
        factor_of = factor_of * one(*cut)
    return factor_of


def normal_values(key, dims, spread, limit, shards=(), held_as=jnp.bfloat16):
    array = spread * jax.random.normal(key, dims, jnp.float32)
    if shards:
        array = array * block_scale(key, dims, shards, -0.22, 0.18)
    return jnp.clip(array, -limit, limit).astype(held_as)


def setup_inputs(seed: int = 0) -> dict:
    seeds = jax.random.split(jax.random.key(seed), 8)
    query = draw_query(jax.random.fold_in(seeds[7], 71), 0)
    keyval = draw_keyval(jax.random.fold_in(seeds[7], 71), 0)
    hidden = normal_values(seeds[2], (2, TIME_TILES, HEIGHT_TILES, WIDTH_TILES, TILE, D), 0.5, 3.0, ((0, 2), (1, 8), (2, 8)))
    out_weight = normal_values(seeds[3], (CHANNELS, D), CHANNELS ** -0.5, 0.15625)
    gate_scale = jnp.clip(jnp.exp(math.log(2.0) - 1.3862944 * jax.random.uniform(seeds[4], (2, D), jnp.float32) ** block_scale(seeds[4], (2, D), ((0, 2),), -0.2, 0.2)), 0.5, 2.0)
    guidance = jnp.clip(jax.random.uniform(seeds[5], (1,), jnp.float32, 1.5, 4.0), 1.5, 4.0)
    counts = draw_counts(jax.random.fold_in(seeds[7], 71), 0)
    return {"query": query, "keyval": keyval, "hidden": hidden, "out_weight": out_weight, "gate_scale": gate_scale, "guidance": guidance, "counts": counts}


masked_score = -1.0e30


def attend_tile(query_tile, key_rows, value_rows, key_live, query_live):
    key_count = key_rows.shape[0]
    queries = query_tile.astype(jnp.float32).reshape(TILE, HEADS, HEAD_DIM)
    key_part = key_rows.astype(jnp.float32).reshape(key_count, HEADS, HEAD_DIM)
    value_part = value_rows.astype(jnp.float32).reshape(key_count, HEADS, HEAD_DIM)
    scores = jnp.einsum("qhd,khd->hqk", queries, key_part) * (HEAD_DIM ** -0.5)
    scores = jnp.where(key_live[None, None, :], scores, masked_score)
    row_max = jnp.max(scores, axis=-1, keepdims=True)
    exponent = jnp.exp(scores - row_max)
    probs = (exponent / jnp.sum(exponent, axis=-1, keepdims=True)).astype(jnp.bfloat16)
    mixed = jnp.einsum("hqk,khd->qhd", probs.astype(jnp.float32), value_part)
    mixed = mixed * query_live[:, None, None]
    return mixed.reshape(TILE, HEADS * HEAD_DIM).astype(jnp.bfloat16)


def reference(query, keyval, hidden, out_weight, gate_scale, guidance, counts):
    tiles = TIME_TILES * HEIGHT_TILES * WIDTH_TILES
    span = min(3, WIDTH_TILES)
    flat_query = query.reshape(2 * tiles, TILE, CHANNELS)
    flat_keyval = keyval.reshape(2, 2 * tiles, TILE, CHANNELS)
    padded_counts = jnp.pad(counts, 1)
    position = jnp.arange(TILE, dtype=jnp.int32)
    step_time = jnp.broadcast_to(jnp.arange(3, dtype=jnp.int32)[:, None, None], (3, 3, span)).reshape(-1)
    step_height = jnp.broadcast_to(jnp.arange(3, dtype=jnp.int32)[None, :, None], (3, 3, span)).reshape(-1)
    step_width = jnp.broadcast_to(jnp.arange(span, dtype=jnp.int32)[None, None, :], (3, 3, span)).reshape(-1)

    def one_tile(tile_index):
        branch = tile_index // tiles
        tile_flat = tile_index % tiles
        time_at = tile_flat // (HEIGHT_TILES * WIDTH_TILES)
        height_at = (tile_flat // WIDTH_TILES) % HEIGHT_TILES
        width_at = tile_flat % WIDTH_TILES
        width_start = jnp.clip(width_at - 1, 0, WIDTH_TILES - span)
        key_time = time_at + step_time - 1
        key_height = height_at + step_height - 1
        key_width = width_start + step_width
        live_count = padded_counts[key_time + 1, key_height + 1, key_width + 1]
        live_count = jnp.where(jnp.abs(key_width - width_at) <= 1, live_count, 0)
        source = branch * tiles + (jnp.clip(key_time, 0, TIME_TILES - 1) * HEIGHT_TILES
                                   + jnp.clip(key_height, 0, HEIGHT_TILES - 1)) * WIDTH_TILES + key_width
        source = source.astype(jnp.int32)
        key_rows = flat_keyval[0][source].reshape(9 * span * TILE, CHANNELS)
        value_rows = flat_keyval[1][source].reshape(9 * span * TILE, CHANNELS)
        key_live = (position[None, :] < live_count[:, None]).reshape(9 * span * TILE)
        own_count = padded_counts[time_at + 1, height_at + 1, width_at + 1]
        query_live = (position < own_count).astype(jnp.float32)
        return attend_tile(flat_query[tile_index], key_rows, value_rows, key_live, query_live)

    attended = lax.map(one_tile, jnp.arange(2 * tiles, dtype=jnp.int32))
    attended = attended.reshape(2, tiles * TILE, CHANNELS)
    flat_hidden = hidden.reshape(2, tiles * TILE, D)
    predictions = []
    for branch in range(2):
        projected = jnp.dot(attended[branch], out_weight, preferred_element_type=jnp.float32)
        predictions.append((flat_hidden[branch].astype(jnp.float32) + gate_scale[branch][None, :] * projected).astype(jnp.bfloat16))
    cond_pred = predictions[0].astype(jnp.float32)
    uncond_pred = predictions[1].astype(jnp.float32)
    guided = uncond_pred + guidance[0] * (cond_pred - uncond_pred)
    return guided.astype(jnp.bfloat16).reshape(TIME_TILES, HEIGHT_TILES, WIDTH_TILES, TILE, D)
```

```python
import functools
import math

import jax
import jax.numpy as jnp
from jax import lax
from jax.experimental import pallas as pl
from jax.experimental.pallas import tpu as pltpu
from jax.sharding import PartitionSpec as P

HEAD_DIM = 128
GROUP = 2
DEPTH = 2
CHUNKS = 4
MASKED = -1e30
MESH = pl.DeviceIdType.MESH


def kernel(
    query, keyval, hidden, weight, gate, guidance, counts, out,
    q_buf, kv_buf, w_buf, hid_buf, o_own, o_out, o_in, l_own, l_out, l_in,
    acc, pred_out, pred_in, result,
    kv_send, kv_recv, q_send, q_recv, o_send, o_recv, l_send, l_recv,
    p_send, p_recv, kv_sem, q_sem, w_sem, hid_sem, out_sem,
):
    rows, channels = query.shape[4], query.shape[5]
    width = GROUP * HEAD_DIM
    groups = channels // width
    model = hidden.shape[5]
    half = model // 2
    scale = HEAD_DIM**-0.5 * math.log2(math.e)

    c, t, h = lax.axis_index("cfg"), lax.axis_index("tm"), lax.axis_index("height")
    times, heights = lax.axis_size("tm"), lax.axis_size("height")
    has_left, has_right = t > 0, t < times - 1
    has_up, has_down = h > 0, h < heights - 1
    left, right, up, down = {"tm": t - 1}, {"tm": t + 1}, {"height": h - 1}, {"height": h + 1}
    other = {"cfg": 1 - c}

    def cols(g):
        return pl.ds(pl.multiple_of(g * width, width), width)

    def kv_local(g):
        return pltpu.make_async_copy(
            keyval.at[:, 0, 0, 0, 0, :, cols(g)], kv_buf.at[1, g], kv_sem.at[g]
        )

    def q_local(g):
        return pltpu.make_async_copy(
            query.at[0, 0, 0, 0, :, cols(g)], q_buf.at[1, g], q_sem.at[g]
        )

    def kv_copy(side, g):
        return pltpu.make_async_remote_copy(
            keyval.at[:, 0, 0, 0, 0, :, cols(g)],
            kv_buf.at[2 - 2 * side, g],
            kv_send.at[side, g],
            kv_recv.at[1 - side, g],
            device_id=(left, right)[side],
            device_id_type=MESH,
        )

    def q_copy(side, g):
        return pltpu.make_async_remote_copy(
            query.at[0, 0, 0, 0, :, cols(g)],
            q_buf.at[2 - 2 * side, g],
            q_send.at[side, g],
            q_recv.at[1 - side, g],
            device_id=(up, down)[side],
            device_id_type=MESH,
        )

    def o_copy(side, g):
        return pltpu.make_async_remote_copy(
            o_out.at[side, g],
            o_in.at[1 - side, g],
            o_send.at[side, g],
            o_recv.at[1 - side, g],
            device_id=(up, down)[side],
            device_id_type=MESH,
        )

    def l_copy(side, g):
        return pltpu.make_async_remote_copy(
            l_out.at[side, g],
            l_in.at[1 - side, g],
            l_send.at[side, g],
            l_recv.at[1 - side, g],
            device_id=(up, down)[side],
            device_id_type=MESH,
        )

    chunk = rows // CHUNKS

    def p_copy(k):
        piece = pl.ds(pl.multiple_of(k * chunk, chunk), chunk)
        return pltpu.make_async_remote_copy(
            pred_out.at[piece],
            pred_in.at[piece],
            p_send.at[k],
            p_recv.at[k],
            device_id=other,
            device_id_type=MESH,
        )

    has_tm, has_height = (has_left, has_right), (has_up, has_down)

    w_copy = pltpu.make_async_copy(weight, w_buf, w_sem)
    hid_copy = pltpu.make_async_copy(hidden.at[0, 0, 0, 0], hid_buf, hid_sem)
    for g in range(groups):
        kv_local(g).start()
        q_local(g).start()

    barrier = pltpu.get_barrier_semaphore()
    near = jnp.int32(1)
    pl.semaphore_signal(barrier, inc=1, device_id=other, device_id_type=MESH)
    for present, device in (
        (has_left, left), (has_right, right), (has_up, up), (has_down, down)
    ):
        near = near + present.astype(jnp.int32)

        @pl.when(present)
        def _():
            pl.semaphore_signal(barrier, inc=1, device_id=device, device_id_type=MESH)

    pl.semaphore_wait(barrier, near)

    for g in range(DEPTH):
        for side in range(2):
            pl.when(has_height[side])(q_copy(side, g).start)
            pl.when(has_tm[side])(kv_copy(side, g).start)
    w_copy.start()
    hid_copy.start()

    for side in range(2):

        @pl.when(jnp.logical_not(has_tm[side]))
        def _():
            kv_buf[2 * side] = jnp.zeros(kv_buf.shape[1:], kv_buf.dtype)

        @pl.when(jnp.logical_not(has_height[side]))
        def _():
            o_in[side] = jnp.zeros(o_in.shape[1:], o_in.dtype)
            l_in[side] = jnp.full(l_in.shape[1:], MASKED, l_in.dtype)

    position = lax.broadcasted_iota(jnp.int32, (1, rows), 1)
    live = []
    for step in (-1, 0, 1):
        at = jnp.clip(t + step, 0, times - 1)
        inside = (t + step >= 0) & (t + step < times)
        live.append(position < jnp.where(inside, counts[at, h, 0], 0))
    own_count = counts[t, h, 0]
    query_live = (
        lax.broadcasted_iota(jnp.int32, (rows, HEAD_DIM), 0) < own_count
    ).astype(jnp.float32)
    low_lanes = lax.broadcasted_iota(jnp.int32, (rows, HEAD_DIM), 1) < HEAD_DIM // 2
    ones = jnp.ones((rows, HEAD_DIM), jnp.bfloat16)

    def attend_head(tile, g, j):
        at = slice(j * HEAD_DIM, (j + 1) * HEAD_DIM)
        q = q_buf[tile, g, :, at]
        scores = []
        for i in range(3):
            s = lax.dot_general(
                q, kv_buf[i, g, 0, :, at], (((1,), (1,)), ((), ())),
                preferred_element_type=jnp.float32,
            )
            scores.append(jnp.where(live[i], s, MASKED))
        top = jnp.maximum(jnp.maximum(scores[0], scores[1]), scores[2])
        top = jnp.max(top, axis=1, keepdims=True)
        mixed = jnp.zeros((rows, 2 * HEAD_DIM), jnp.float32)
        for i in range(3):
            p = jnp.exp2((scores[i] - top) * scale).astype(jnp.bfloat16)
            v = jnp.concatenate([kv_buf[i, g, 1, :, at], ones], axis=1)
            mixed = mixed + jnp.dot(p, v, preferred_element_type=jnp.float32)
        total = mixed[:, HEAD_DIM:]
        result = mixed[:, :HEAD_DIM] / total
        return result, top * scale + jnp.log(total) * math.log2(math.e)

    def attend(g):
        def one(tile):
            heads = [attend_head(tile, g, j) for j in range(GROUP)]
            mixed = jnp.concatenate([x for x, _ in heads], axis=1)
            return mixed, jnp.where(low_lanes, heads[0][1], heads[1][1])

        for side in range(2):

            @pl.when(has_height[side])
            def _():
                q_copy(1 - side, g).wait_recv()
                mixed, level = one(2 * side)
                o_out[side, g] = mixed.astype(jnp.bfloat16)
                l_out[side, g] = level
                o_copy(side, g).start()
                l_copy(side, g).start()

        mixed, level = one(1)
        o_own[g] = mixed
        l_own[g] = level

    def combine(g):
        for side in range(2):

            @pl.when(has_height[side])
            def _():
                o_copy(1 - side, g).wait_recv()
                l_copy(1 - side, g).wait_recv()

        levels = [l_in[0, g], l_own[g], l_in[1, g]]
        top = jnp.maximum(jnp.maximum(levels[0], levels[1]), levels[2])
        shares = [jnp.exp2(x - top) for x in levels]
        total = shares[0] + shares[1] + shares[2]
        shares = [x / total * query_live for x in shares]
        parts = []
        for j in range(GROUP):
            at = slice(j * HEAD_DIM, (j + 1) * HEAD_DIM)
            lane = j * HEAD_DIM // 2
            parts.append(
                shares[0][:, lane : lane + 1] * o_in[0, g, :, at].astype(jnp.float32)
                + shares[1][:, lane : lane + 1] * o_own[g, :, at]
                + shares[2][:, lane : lane + 1] * o_in[1, g, :, at].astype(jnp.float32)
            )
        attended = jnp.concatenate(parts, axis=1).astype(jnp.bfloat16)
        block = 512
        depth = pl.ds(pl.multiple_of(g * width, width), width)

        def add(k, carry):
            at = pl.ds(pl.multiple_of(k * block, block), block)
            acc[:, at] += jnp.dot(
                attended, w_buf[depth, at], preferred_element_type=jnp.float32
            )
            return carry

        lax.fori_loop(0, model // block, add, 0)

    acc[...] = jnp.zeros_like(acc)
    w_copy.wait()

    def step(g, carry):
        for side in range(2):

            @pl.when(has_tm[side])
            def _():
                kv_copy(1 - side, g).wait_recv()

        kv_local(g).wait()
        q_local(g).wait()

        @pl.when(g + DEPTH < groups)
        def _():
            for side in range(2):
                pl.when(has_height[side])(q_copy(side, g + DEPTH).start)
                pl.when(has_tm[side])(kv_copy(side, g + DEPTH).start)

        attend(g)

        @pl.when(g > 0)
        def _():
            combine(g - 1)

        return carry

    lax.fori_loop(0, groups, step, 0)
    combine(groups - 1)
    hid_copy.wait()

    def predict(k, side):
        piece = pl.ds(pl.multiple_of(k * chunk, chunk), chunk)
        at = pl.ds(pl.multiple_of(side * half, half), half)
        stream = hid_buf[piece, at].astype(jnp.float32)
        return (stream + gate[:, at] * acc[piece, at]).astype(jnp.bfloat16)

    for k in range(CHUNKS):
        pred_out[k * chunk : (k + 1) * chunk] = predict(k, 1 - c)
        p_copy(k).start()
    for k in range(CHUNKS):
        piece = slice(k * chunk, (k + 1) * chunk)
        mine = predict(k, c).astype(jnp.float32)
        p_copy(k).wait_recv()
        theirs = pred_in[piece].astype(jnp.float32)
        cond = jnp.where(c == 0, mine, theirs)
        uncond = jnp.where(c == 0, theirs, mine)
        result[piece] = (uncond + guidance[0] * (cond - uncond)).astype(jnp.bfloat16)
        pltpu.make_async_copy(result.at[piece], out.at[0, 0, 0, piece], out_sem.at[k]).start()
    for k in range(CHUNKS):
        piece = slice(k * chunk, (k + 1) * chunk)
        pltpu.make_async_copy(result.at[piece], out.at[0, 0, 0, piece], out_sem.at[k]).wait()
        p_copy(k).wait_send()

    def drain(g, carry):
        for side in range(2):

            @pl.when(has_tm[side])
            def _():
                kv_copy(side, g).wait_send()

            @pl.when(has_height[side])
            def _():
                q_copy(side, g).wait_send()
                o_copy(side, g).wait_send()
                l_copy(side, g).wait_send()

        return carry

    lax.fori_loop(0, groups, drain, 0)


def on_device(query, keyval, hidden, out_weight, gate_scale, guidance, counts):
    rows, channels = query.shape[4], query.shape[5]
    model = hidden.shape[5]
    width = GROUP * HEAD_DIM
    groups = channels // width
    bf16, f32, dma = jnp.bfloat16, jnp.float32, pltpu.SemaphoreType.DMA
    anywhere = pl.BlockSpec(memory_space=pl.ANY)
    vmem = pl.BlockSpec(memory_space=pltpu.VMEM)
    smem = pl.BlockSpec(memory_space=pltpu.SMEM)
    return pl.pallas_call(
        kernel,
        out_shape=jax.ShapeDtypeStruct((1, 1, 1, rows, model // 2), bf16),
        in_specs=[anywhere, anywhere, anywhere, anywhere, vmem, smem, smem],
        out_specs=anywhere,
        scratch_shapes=[
            pltpu.VMEM((3, groups, rows, width), bf16),
            pltpu.VMEM((3, groups, 2, rows, width), bf16),
            pltpu.VMEM((channels, model), bf16),
            pltpu.VMEM((rows, model), bf16),
            pltpu.VMEM((groups, rows, width), f32),
            pltpu.VMEM((2, groups, rows, width), bf16),
            pltpu.VMEM((2, groups, rows, width), bf16),
            pltpu.VMEM((groups, rows, HEAD_DIM), f32),
            pltpu.VMEM((2, groups, rows, HEAD_DIM), f32),
            pltpu.VMEM((2, groups, rows, HEAD_DIM), f32),
            pltpu.VMEM((rows, model), f32),
            pltpu.VMEM((rows, model // 2), bf16),
            pltpu.VMEM((rows, model // 2), bf16),
            pltpu.VMEM((rows, model // 2), bf16),
        ]
        + [dma((2, groups))] * 8
        + [dma((CHUNKS,))] * 2
        + [dma((groups,))] * 2
        + [dma, dma, dma((CHUNKS,))],
        compiler_params=pltpu.CompilerParams(
            collective_id=0, has_side_effects=True, vmem_limit_bytes=60 * 2**20
        ),
    )(query, keyval, hidden, out_weight, gate_scale, guidance, counts)


def solution(mesh):
    return jax.shard_map(
        on_device,
        mesh=mesh,
        in_specs=(
            P("cfg", "tm", "height", None, None, None),
            P(None, "cfg", "tm", "height", None, None, None),
            P("cfg", "tm", "height", None, None, None),
            P(),
            P("cfg", None),
            P(),
            P(),
        ),
        out_specs=P("tm", "height", None, None, "cfg"),
        check_vma=False,
    )
```

```python
import functools
import math

import jax
import jax.numpy as jnp
from jax import lax
from jax.experimental import pallas as pl
from jax.experimental.pallas import tpu as pltpu
from jax.sharding import PartitionSpec as P

HEAD_DIM = 128
GROUP = 2
DEPTH = 4
EARLY = 288
CHUNKS = 2
MASKED = -1e30
MESH = pl.DeviceIdType.MESH


def kernel(
    query, keyval, hidden, weight, gate, guidance, counts, out,
    q_buf, kv_buf, w_buf, hid_buf, o_own, o_out, o_in, l_own, l_out, l_in,
    acc, acc_late, acc_in, pred_out, pred_in, a_out, a_in, hid_in, gate_in, result,
    kv_send, kv_recv, q_send, q_recv, o_send, o_recv, l_send, l_recv,
    a_send, a_recv, p_send, p_recv, x_send, x_recv, kv_sem, q_sem, w_sem, hid_sem, out_sem,
):
    rows, channels = query.shape[4], query.shape[5]
    width = GROUP * HEAD_DIM
    groups = channels // width
    model = hidden.shape[5]
    half = model // 2
    scale = HEAD_DIM**-0.5 * math.log2(math.e)

    c, t, h = lax.axis_index("cfg"), lax.axis_index("tm"), lax.axis_index("height")
    times, heights = lax.axis_size("tm"), lax.axis_size("height")
    has_left, has_right = t > 0, t < times - 1
    has_up, has_down = h > 0, h < heights - 1
    left, right, up, down = {"tm": t - 1}, {"tm": t + 1}, {"height": h - 1}, {"height": h + 1}
    other = {"cfg": 1 - c}

    def cols(g):
        return pl.ds(pl.multiple_of(g * width, width), width)

    def kv_local(g):
        return pltpu.make_async_copy(
            keyval.at[:, 0, 0, 0, 0, :, cols(g)], kv_buf.at[1, g], kv_sem.at[g]
        )

    def q_local(g):
        return pltpu.make_async_copy(
            query.at[0, 0, 0, 0, :, cols(g)], q_buf.at[1, g], q_sem.at[g]
        )

    middle = times // 2

    def relayed(g):
        return (g == 1) | (g == 2) | (g == 3)

    def kv_copy(side, g):
        by = relayed(g) & (t == (middle, middle - 1)[side])
        return pltpu.make_async_remote_copy(
            keyval.at[:, 0, 0, 0, 0, :, cols(g)],
            kv_buf.at[jnp.where(by, 2 * side, 2 - 2 * side), g],
            kv_send.at[side, g],
            kv_recv.at[jnp.where(by, side, 1 - side), g],
            device_id={"tm": jnp.where(by, (0, times - 1)[side], t + (-1, 1)[side])},
            device_id_type=MESH,
        )

    def kv_forward(side, g):
        return pltpu.make_async_remote_copy(
            kv_buf.at[2 * side, g],
            kv_buf.at[2 - 2 * side, g],
            kv_send.at[side, g],
            kv_recv.at[1 - side, g],
            device_id={"tm": (middle - 1, middle)[side]},
            device_id_type=MESH,
        )

    def kv_arrival(side, g):
        return pltpu.make_async_remote_copy(
            kv_buf.at[2 * side, g],
            kv_buf.at[2 * side, g],
            kv_send.at[side, g],
            kv_recv.at[side, g],
            device_id=other,
            device_id_type=MESH,
        )

    def q_copy(side, g):
        return pltpu.make_async_remote_copy(
            query.at[0, 0, 0, 0, :, cols(g)],
            q_buf.at[2 - 2 * side, g],
            q_send.at[side, g],
            q_recv.at[1 - side, g],
            device_id=(up, down)[side],
            device_id_type=MESH,
        )

    def o_copy(side, g):
        return pltpu.make_async_remote_copy(
            o_out.at[side, g],
            o_in.at[1 - side, g],
            o_send.at[side, g],
            o_recv.at[1 - side, g],
            device_id=(up, down)[side],
            device_id_type=MESH,
        )

    def l_copy(side, g):
        return pltpu.make_async_remote_copy(
            l_out.at[side, g],
            l_in.at[1 - side, g],
            l_send.at[side, g],
            l_recv.at[1 - side, g],
            device_id=(up, down)[side],
            device_id_type=MESH,
        )

    def a_copy(g):
        return pltpu.make_async_remote_copy(
            a_out.at[:, cols(g)],
            a_in.at[:, cols(g)],
            a_send.at[g],
            a_recv.at[g],
            device_id=other,
            device_id_type=MESH,
        )

    late = rows - EARLY
    chunk = late // CHUNKS

    def p_copy(k):
        piece = pl.ds(k * chunk, chunk)
        return pltpu.make_async_remote_copy(
            pred_out.at[piece],
            pred_in.at[piece],
            p_send.at[k],
            p_recv.at[k],
            device_id=other,
            device_id_type=MESH,
        )

    mine = pl.ds(pl.multiple_of(c * half, half), half)
    theirs = pl.ds(pl.multiple_of((1 - c) * half, half), half)
    hid_swap = pltpu.make_async_remote_copy(
        hidden.at[0, 0, 0, 0, :EARLY, theirs],
        hid_in,
        x_send.at[0],
        x_recv.at[0],
        device_id=other,
        device_id_type=MESH,
    )
    gate_swap = pltpu.make_async_remote_copy(
        gate, gate_in, x_send.at[1], x_recv.at[1], device_id=other, device_id_type=MESH
    )

    has_tm, has_height = (has_left, has_right), (has_up, has_down)

    w_copy = pltpu.make_async_copy(weight, w_buf, w_sem)
    hid_copy = pltpu.make_async_copy(hidden.at[0, 0, 0, 0], hid_buf, hid_sem)
    for g in range(groups):
        kv_local(g).start()
        q_local(g).start()

    barrier = pltpu.get_barrier_semaphore()
    near = jnp.int32(1)
    pl.semaphore_signal(barrier, inc=1, device_id=other, device_id_type=MESH)
    for present, device in (
        (has_left, left), (has_right, right), (has_up, up), (has_down, down)
    ):
        near = near + present.astype(jnp.int32)

        @pl.when(present)
        def _():
            pl.semaphore_signal(barrier, inc=1, device_id=device, device_id_type=MESH)

    for at, far in (
        (0, middle - 1), (0, middle), (middle - 1, 0),
        (middle, 0), (times - 1, middle - 1), (times - 1, middle),
        (middle - 1, times - 1), (middle, times - 1),
    ):
        near = near + (t == at).astype(jnp.int32)

        @pl.when(t == at)
        def _():
            pl.semaphore_signal(barrier, inc=1, device_id={"tm": far}, device_id_type=MESH)

    pl.semaphore_wait(barrier, near)

    for g in range(DEPTH):
        for side in range(2):
            pl.when(has_height[side])(q_copy(side, g).start)
            pl.when(has_tm[side])(kv_copy(side, g).start)
    w_copy.start()
    hid_swap.start()
    gate_swap.start()
    hid_copy.start()

    for side in range(2):

        @pl.when(jnp.logical_not(has_tm[side]))
        def _():
            for g in range(groups):
                if not relayed(g):
                    kv_buf[2 * side, g] = jnp.zeros(kv_buf.shape[2:], kv_buf.dtype)

        @pl.when(jnp.logical_not(has_height[side]))
        def _():
            o_in[side] = jnp.zeros(o_in.shape[1:], o_in.dtype)
            l_in[side] = jnp.full(l_in.shape[1:], MASKED, l_in.dtype)

    position = lax.broadcasted_iota(jnp.int32, (1, rows), 1)
    live = []
    for step in (-1, 0, 1):
        at = jnp.clip(t + step, 0, times - 1)
        inside = (t + step >= 0) & (t + step < times)
        live.append(position < jnp.where(inside, counts[at, h, 0], 0))
    own_count = counts[t, h, 0]
    query_live = (
        lax.broadcasted_iota(jnp.int32, (rows, HEAD_DIM), 0) < own_count
    ).astype(jnp.float32)
    low_lanes = lax.broadcasted_iota(jnp.int32, (rows, HEAD_DIM), 1) < HEAD_DIM // 2
    ones = jnp.ones((rows, HEAD_DIM), jnp.bfloat16)

    def attend_head(tile, g, j):
        at = slice(j * HEAD_DIM, (j + 1) * HEAD_DIM)
        q = q_buf[tile, g, :, at]
        scores = []
        for i in range(3):
            s = lax.dot_general(
                q, kv_buf[i, g, 0, :, at], (((1,), (1,)), ((), ())),
                preferred_element_type=jnp.float32,
            )
            scores.append(jnp.where(live[i], s, MASKED))
        top = jnp.maximum(jnp.maximum(scores[0], scores[1]), scores[2])
        top = jnp.max(top, axis=1, keepdims=True)
        mixed = jnp.zeros((rows, 2 * HEAD_DIM), jnp.float32)
        for i in range(3):
            p = jnp.exp2((scores[i] - top) * scale).astype(jnp.bfloat16)
            v = jnp.concatenate([kv_buf[i, g, 1, :, at], ones], axis=1)
            mixed = mixed + jnp.dot(p, v, preferred_element_type=jnp.float32)
        total = mixed[:, HEAD_DIM:]
        result = mixed[:, :HEAD_DIM] / total
        return result, top * scale + jnp.log(total) * math.log2(math.e)

    def attend(g):
        def one(tile):
            heads = [attend_head(tile, g, j) for j in range(GROUP)]
            mixed = jnp.concatenate([x for x, _ in heads], axis=1)
            return mixed, jnp.where(low_lanes, heads[0][1], heads[1][1])

        for side in range(2):

            @pl.when(has_height[side])
            def _():
                q_copy(1 - side, g).wait_recv()
                mixed, level = one(2 * side)
                o_out[side, g] = mixed.astype(jnp.bfloat16)
                l_out[side, g] = level
                o_copy(side, g).start()
                l_copy(side, g).start()

        mixed, level = one(1)
        o_own[g] = mixed
        l_own[g] = level

    def combine(g):
        for side in range(2):

            @pl.when(has_height[side])
            def _():
                o_copy(1 - side, g).wait_recv()
                l_copy(1 - side, g).wait_recv()

        levels = [l_in[0, g], l_own[g], l_in[1, g]]
        top = jnp.maximum(jnp.maximum(levels[0], levels[1]), levels[2])
        shares = [jnp.exp2(x - top) for x in levels]
        total = shares[0] + shares[1] + shares[2]
        shares = [x / total * query_live for x in shares]
        parts = []
        for j in range(GROUP):
            at = slice(j * HEAD_DIM, (j + 1) * HEAD_DIM)
            lane = j * HEAD_DIM // 2
            parts.append(
                shares[0][:, lane : lane + 1] * o_in[0, g, :, at].astype(jnp.float32)
                + shares[1][:, lane : lane + 1] * o_own[g, :, at]
                + shares[2][:, lane : lane + 1] * o_in[1, g, :, at].astype(jnp.float32)
            )
        attended = jnp.concatenate(parts, axis=1).astype(jnp.bfloat16)
        a_out[:, cols(g)] = attended[:EARLY]
        a_copy(g).start()
        project(g, attended[EARLY:], acc_late, (1 - c) * half)
        project(g, attended, acc, c * half)

    def project(g, attended, total, first):
        block = 512
        depth = pl.ds(pl.multiple_of(g * width, width), width)

        def add(k, carry):
            at = pl.ds(pl.multiple_of(k * block, block), block)
            column = pl.ds(pl.multiple_of(first + k * block, block), block)
            total[:, at] += jnp.dot(
                attended, w_buf[depth, column], preferred_element_type=jnp.float32
            )
            return carry

        lax.fori_loop(0, half // block, add, 0)

    acc_late[...] = jnp.zeros_like(acc_late)
    acc[...] = jnp.zeros_like(acc)
    w_copy.wait()

    def step(g, carry):
        for side in range(2):
            end = t == (0, times - 1)[side]
            pl.when(has_tm[side])(kv_arrival(side, g).wait_recv)

            @pl.when(end & relayed(g + 1))
            def _():
                kv_arrival(side, g + 1).wait_recv()
                kv_forward(side, g + 1).start()

        kv_local(g).wait()
        q_local(g).wait()

        @pl.when(g + DEPTH < groups)
        def _():
            for side in range(2):
                pl.when(has_height[side])(q_copy(side, g + DEPTH).start)
                pl.when(has_tm[side])(kv_copy(side, g + DEPTH).start)

        attend(g)

        @pl.when(g > 0)
        def _():
            combine(g - 1)

        return carry

    lax.fori_loop(0, groups, step, 0)
    combine(groups - 1)
    hid_copy.wait()
    for k in range(CHUNKS):
        piece = slice(k * chunk, (k + 1) * chunk)
        stream = hid_buf[EARLY + k * chunk : EARLY + (k + 1) * chunk, theirs]
        pred_out[piece] = (
            stream.astype(jnp.float32) + gate[:, theirs] * acc_late[piece]
        ).astype(jnp.bfloat16)
        p_copy(k).start()
    for g in range(groups):
        a_copy(g).wait_recv()

    def project_in(k, carry):
        at = pl.ds(pl.multiple_of(k * 256, 256), 256)
        column = pl.ds(pl.multiple_of(c * half + k * 256, 256), 256)
        acc_in[:, at] = jnp.dot(
            a_in[...], w_buf[:, column], preferred_element_type=jnp.float32
        )
        return carry

    lax.fori_loop(0, half // 256, project_in, 0)
    hid_swap.wait_recv()
    gate_swap.wait_recv()

    def guide(k, size, their_pred):
        piece = pl.ds(k * size, size)
        stream = hid_buf[piece, mine].astype(jnp.float32)
        own = (stream + gate[:, mine] * acc[piece]).astype(jnp.bfloat16).astype(jnp.float32)
        cond = jnp.where(c == 0, own, their_pred)
        uncond = jnp.where(c == 0, their_pred, own)
        result[piece] = (uncond + guidance[0] * (cond - uncond)).astype(jnp.bfloat16)

    def store(k):
        piece = pl.ds(k * chunk, chunk)
        return pltpu.make_async_copy(result.at[piece], out.at[0, 0, 0, piece], out_sem.at[k])

    before = EARLY // chunk
    for k in range(before):
        piece = slice(k * chunk, (k + 1) * chunk)
        pred = hid_in[piece].astype(jnp.float32) + gate_in[:, mine] * acc_in[piece]
        guide(k, chunk, pred.astype(jnp.bfloat16).astype(jnp.float32))
        store(k).start()
    for k in range(CHUNKS):
        p_copy(k).wait_recv()
        guide(before + k, chunk, pred_in[k * chunk : (k + 1) * chunk].astype(jnp.float32))
        store(before + k).start()
    for k in range(before + CHUNKS):
        store(k).wait()
    for k in range(CHUNKS):
        p_copy(k).wait_send()
    hid_swap.wait_send()
    gate_swap.wait_send()

    def drain(g, carry):
        a_copy(g).wait_send()
        for side in range(2):
            end = t == (0, times - 1)[side]
            pl.when(has_tm[side])(kv_copy(side, g).wait_send)
            pl.when(end & relayed(g))(kv_forward(side, g).wait_send)

            @pl.when(has_height[side])
            def _():
                q_copy(side, g).wait_send()
                o_copy(side, g).wait_send()
                l_copy(side, g).wait_send()

        return carry

    lax.fori_loop(0, groups, drain, 0)


def on_device(query, keyval, hidden, out_weight, gate_scale, guidance, counts):
    rows, channels = query.shape[4], query.shape[5]
    model = hidden.shape[5]
    width = GROUP * HEAD_DIM
    groups = channels // width
    bf16, f32, dma = jnp.bfloat16, jnp.float32, pltpu.SemaphoreType.DMA
    anywhere = pl.BlockSpec(memory_space=pl.ANY)
    vmem = pl.BlockSpec(memory_space=pltpu.VMEM)
    smem = pl.BlockSpec(memory_space=pltpu.SMEM)
    return pl.pallas_call(
        kernel,
        out_shape=jax.ShapeDtypeStruct((1, 1, 1, rows, model // 2), bf16),
        in_specs=[anywhere, anywhere, anywhere, anywhere, vmem, smem, smem],
        out_specs=anywhere,
        scratch_shapes=[
            pltpu.VMEM((3, groups, rows, width), bf16),
            pltpu.VMEM((3, groups, 2, rows, width), bf16),
            pltpu.VMEM((channels, model), bf16),
            pltpu.VMEM((rows, model), bf16),
            pltpu.VMEM((groups, rows, width), f32),
            pltpu.VMEM((2, groups, rows, width), bf16),
            pltpu.VMEM((2, groups, rows, width), bf16),
            pltpu.VMEM((groups, rows, HEAD_DIM), f32),
            pltpu.VMEM((2, groups, rows, HEAD_DIM), f32),
            pltpu.VMEM((2, groups, rows, HEAD_DIM), f32),
            pltpu.VMEM((rows, model // 2), f32),
            pltpu.VMEM((rows - EARLY, model // 2), f32),
            pltpu.VMEM((EARLY, model // 2), f32),
            pltpu.VMEM((rows - EARLY, model // 2), bf16),
            pltpu.VMEM((rows - EARLY, model // 2), bf16),
            pltpu.VMEM((EARLY, channels), bf16),
            pltpu.VMEM((EARLY, channels), bf16),
            pltpu.VMEM((EARLY, model // 2), bf16),
            pltpu.VMEM((1, model), f32),
            pltpu.VMEM((rows, model // 2), bf16),
        ]
        + [dma((2, groups))] * 8
        + [dma((groups,))] * 2
        + [dma((CHUNKS,))] * 2
        + [dma((2,))] * 2
        + [dma((groups,))] * 2
        + [dma, dma, dma((rows * CHUNKS // (rows - EARLY),))],
        compiler_params=pltpu.CompilerParams(
            collective_id=0, has_side_effects=True, vmem_limit_bytes=60 * 2**20
        ),
    )(query, keyval, hidden, out_weight, gate_scale, guidance, counts)


def solution(mesh):
    return jax.shard_map(
        on_device,
        mesh=mesh,
        in_specs=(
            P("cfg", "tm", "height", None, None, None),
            P(None, "cfg", "tm", "height", None, None, None),
            P("cfg", "tm", "height", None, None, None),
            P(),
            P("cfg", None),
            P(),
            P(),
        ),
        out_specs=P("tm", "height", None, None, "cfg"),
        check_vma=False,
    )
```

```python
import functools
import math

import jax
import jax.numpy as jnp
from jax import lax
from jax.experimental import pallas as pl
from jax.experimental.pallas import tpu as pltpu
from jax.sharding import PartitionSpec as P

HEAD_DIM = 128
PAIR = 2
DEPTH = 8
EARLY = 256
CHUNKS = 2
MASKED = -1e30
MESH = pl.DeviceIdType.MESH


def kernel(
    query, keyval, hidden, weight, gate, guidance, counts, out,
    q_buf, kv_buf, w_buf, hid_buf, o_own, o_out, o_in, l_own, l_out, l_in,
    acc, acc_late, acc_in, pred_out, pred_in, a_out, a_in, hid_in, gate_in, result,
    kv_send, kv_recv, q_send, q_recv, o_send, o_recv, l_send, l_recv,
    a_send, a_recv, p_send, p_recv, x_send, x_recv, kv_sem, q_sem, w_sem, hid_sem, out_sem,
):
    rows, channels = query.shape[4], query.shape[5]
    heads = channels // HEAD_DIM
    pairs, width = heads // PAIR, PAIR * HEAD_DIM
    model = hidden.shape[5]
    half = model // 2
    scale = HEAD_DIM**-0.5 * math.log2(math.e)

    c, t, h = lax.axis_index("cfg"), lax.axis_index("tm"), lax.axis_index("height")
    times, heights = lax.axis_size("tm"), lax.axis_size("height")
    has_left, has_right = t > 0, t < times - 1
    has_up, has_down = h > 0, h < heights - 1
    left, right, up, down = {"tm": t - 1}, {"tm": t + 1}, {"height": h - 1}, {"height": h + 1}
    other = {"cfg": 1 - c}

    def cols(g):
        return pl.ds(pl.multiple_of(g * HEAD_DIM, HEAD_DIM), HEAD_DIM)

    def pair_cols(n):
        return pl.ds(pl.multiple_of(n * width, width), width)

    def kv_slot(slot, g):
        return kv_buf.at[g, :, pl.ds(pl.multiple_of(slot * rows, rows), rows)]

    def q_slot(slot, g):
        return q_buf.at[g, pl.ds(pl.multiple_of(slot * rows, rows), rows)]

    def kv_local(g):
        return pltpu.make_async_copy(
            keyval.at[:, 0, 0, 0, 0, :, cols(g)], kv_slot(1, g), kv_sem.at[g]
        )

    def q_local(g):
        return pltpu.make_async_copy(
            query.at[0, 0, 0, 0, :, cols(g)], q_slot(1, g), q_sem.at[g]
        )

    middle = times // 2

    def relayed(g):
        return (g >= heads // 6) & (g < heads * 2 // 3)

    def kv_copy(side, g):
        by = relayed(g) & (t == (middle, middle - 1)[side])
        return pltpu.make_async_remote_copy(
            keyval.at[:, 0, 0, 0, 0, :, cols(g)],
            kv_slot(jnp.where(by, 2 * side, 2 - 2 * side), g),
            kv_send.at[side, g],
            kv_recv.at[jnp.where(by, side, 1 - side), g],
            device_id={"tm": jnp.where(by, (0, times - 1)[side], t + (-1, 1)[side])},
            device_id_type=MESH,
        )

    def kv_forward(side, g):
        return pltpu.make_async_remote_copy(
            kv_slot(2 * side, g),
            kv_slot(2 - 2 * side, g),
            kv_send.at[side, g],
            kv_recv.at[1 - side, g],
            device_id={"tm": (middle - 1, middle)[side]},
            device_id_type=MESH,
        )

    def kv_arrival(side, g):
        return pltpu.make_async_remote_copy(
            kv_slot(2 * side, g),
            kv_slot(2 * side, g),
            kv_send.at[side, g],
            kv_recv.at[side, g],
            device_id=other,
            device_id_type=MESH,
        )

    def q_copy(side, g):
        return pltpu.make_async_remote_copy(
            query.at[0, 0, 0, 0, :, cols(g)],
            q_slot(2 - 2 * side, g),
            q_send.at[side, g],
            q_recv.at[1 - side, g],
            device_id=(up, down)[side],
            device_id_type=MESH,
        )

    def o_copy(side, g):
        return pltpu.make_async_remote_copy(
            o_out.at[side, g],
            o_in.at[1 - side, g],
            o_send.at[side, g],
            o_recv.at[1 - side, g],
            device_id=(up, down)[side],
            device_id_type=MESH,
        )

    def l_copy(side, g):
        return pltpu.make_async_remote_copy(
            l_out.at[side, g],
            l_in.at[1 - side, g],
            l_send.at[side, g],
            l_recv.at[1 - side, g],
            device_id=(up, down)[side],
            device_id_type=MESH,
        )

    def a_copy(n):
        return pltpu.make_async_remote_copy(
            a_out.at[:, pair_cols(n)],
            a_in.at[:, pair_cols(n)],
            a_send.at[n],
            a_recv.at[n],
            device_id=other,
            device_id_type=MESH,
        )

    late = rows - EARLY
    chunk = late // CHUNKS

    def p_copy(k):
        piece = pl.ds(k * chunk, chunk)
        return pltpu.make_async_remote_copy(
            pred_out.at[piece],
            pred_in.at[piece],
            p_send.at[k],
            p_recv.at[k],
            device_id=other,
            device_id_type=MESH,
        )

    mine = pl.ds(pl.multiple_of(c * half, half), half)
    theirs = pl.ds(pl.multiple_of((1 - c) * half, half), half)
    hid_swap = pltpu.make_async_remote_copy(
        hidden.at[0, 0, 0, 0, :EARLY, theirs],
        hid_in,
        x_send.at[0],
        x_recv.at[0],
        device_id=other,
        device_id_type=MESH,
    )
    gate_swap = pltpu.make_async_remote_copy(
        gate, gate_in, x_send.at[1], x_recv.at[1], device_id=other, device_id_type=MESH
    )

    has_tm, has_height = (has_left, has_right), (has_up, has_down)

    w_copy = pltpu.make_async_copy(weight, w_buf, w_sem)
    hid_copy = pltpu.make_async_copy(hidden.at[0, 0, 0, 0], hid_buf, hid_sem)
    for g in range(heads):
        kv_local(g).start()
        q_local(g).start()

    barrier = pltpu.get_barrier_semaphore()
    near = jnp.int32(1)
    pl.semaphore_signal(barrier, inc=1, device_id=other, device_id_type=MESH)
    for present, device in (
        (has_left, left), (has_right, right), (has_up, up), (has_down, down)
    ):
        near = near + present.astype(jnp.int32)

        @pl.when(present)
        def _():
            pl.semaphore_signal(barrier, inc=1, device_id=device, device_id_type=MESH)

    for at, far in (
        (0, middle - 1), (0, middle), (middle - 1, 0),
        (middle, 0), (times - 1, middle - 1), (times - 1, middle),
        (middle - 1, times - 1), (middle, times - 1),
    ):
        near = near + (t == at).astype(jnp.int32)

        @pl.when(t == at)
        def _():
            pl.semaphore_signal(barrier, inc=1, device_id={"tm": far}, device_id_type=MESH)

    pl.semaphore_wait(barrier, near)

    for g in range(DEPTH):
        for side in range(2):
            pl.when(has_height[side])(q_copy(side, g).start)
            pl.when(has_tm[side])(kv_copy(side, g).start)
    w_copy.start()
    hid_swap.start()
    gate_swap.start()
    hid_copy.start()

    for side in range(2):

        @pl.when(jnp.logical_not(has_tm[side]))
        def _():
            for g in range(heads):
                if not relayed(g):
                    kv_buf[g, :, 2 * side * rows : (2 * side + 1) * rows] = jnp.zeros(
                        (2, rows, HEAD_DIM), kv_buf.dtype
                    )

        @pl.when(jnp.logical_not(has_height[side]))
        def _():
            q_buf[:, 2 * side * rows : (2 * side + 1) * rows] = jnp.zeros(
                (heads, rows, HEAD_DIM), q_buf.dtype
            )
            o_in[side] = jnp.zeros(o_in.shape[1:], o_in.dtype)
            l_in[side] = jnp.full(l_in.shape[1:], MASKED, l_in.dtype)

    position = lax.broadcasted_iota(jnp.int32, (1, rows), 1)
    live = []
    for step in (-1, 0, 1):
        at = jnp.clip(t + step, 0, times - 1)
        inside = (t + step >= 0) & (t + step < times)
        seen = position < jnp.where(inside, counts[at, 0, h], 0)
        live.append(seen.astype(jnp.int32))
    live = jnp.concatenate(live, axis=1) > 0
    own_count = counts[t, 0, h]
    query_live = (
        lax.broadcasted_iota(jnp.int32, (rows, HEAD_DIM), 0) < own_count
    ).astype(jnp.float32)
    low_lanes = lax.broadcasted_iota(jnp.int32, (rows, HEAD_DIM), 1) < HEAD_DIM // 2
    ones = jnp.ones((3 * rows, HEAD_DIM), jnp.bfloat16)

    def attend_rows(first, size, g):
        scores = lax.dot_general(
            q_buf[g, first : first + size], kv_buf[g, 0], (((1,), (1,)), ((), ())),
            preferred_element_type=jnp.float32,
        )
        scores = jnp.where(live, scores, MASKED)
        top = jnp.max(scores, axis=1, keepdims=True)
        probs = jnp.exp2((scores - top) * scale).astype(jnp.bfloat16)
        values = jnp.concatenate([kv_buf[g, 1], ones], axis=1)
        mixed = jnp.dot(probs, values, preferred_element_type=jnp.float32)
        total = mixed[:, HEAD_DIM:]
        level = top * scale + jnp.log(total) * math.log2(math.e)
        return mixed[:, :HEAD_DIM] / total, level

    def attend(g):
        for side in range(2):
            pl.when(has_height[side])(q_copy(1 - side, g).wait_recv)

        size = 3 * rows // 2
        results = [attend_rows(first, size, g) for first in (0, size)]
        mixed = jnp.concatenate([x for x, _ in results], axis=0)
        level = jnp.concatenate([x for _, x in results], axis=0)
        for side in range(2):
            at = slice(2 * side * rows, (2 * side + 1) * rows)
            o_out[side, g] = mixed[at].astype(jnp.bfloat16)
            l_out[side, g] = jnp.transpose(level[at])[:8]
        o_own[g] = mixed[rows : 2 * rows]
        l_own[g] = level[rows : 2 * rows]
        for side in range(2):

            @pl.when(has_height[side])
            def _():
                o_copy(side, g).start()
                l_copy(side, g).start()

    def combine(n):
        for side in range(2):

            @pl.when(has_height[side])
            def _():
                for j in range(PAIR):
                    o_copy(1 - side, n * PAIR + j).wait_recv()
                    l_copy(1 - side, n * PAIR + j).wait_recv()

        def arrived(side):
            spread = [
                jnp.broadcast_to(l_in[side, n * PAIR + j, :1], (HEAD_DIM // 2, rows))
                for j in range(PAIR)
            ]
            return jnp.transpose(jnp.concatenate(spread, axis=0))

        own_level = jnp.where(low_lanes, l_own[n * PAIR], l_own[n * PAIR + 1])
        levels = [arrived(0), own_level, arrived(1)]
        top = jnp.maximum(jnp.maximum(levels[0], levels[1]), levels[2])
        shares = [jnp.exp2(x - top) for x in levels]
        total = shares[0] + shares[1] + shares[2]
        shares = [x / total * query_live for x in shares]
        parts = []
        for j in range(PAIR):
            lane, g = j * HEAD_DIM // 2, n * PAIR + j
            parts.append(
                shares[0][:, lane : lane + 1] * o_in[0, g].astype(jnp.float32)
                + shares[1][:, lane : lane + 1] * o_own[g]
                + shares[2][:, lane : lane + 1] * o_in[1, g].astype(jnp.float32)
            )
        attended = jnp.concatenate(parts, axis=1).astype(jnp.bfloat16)
        a_out[:, pair_cols(n)] = attended[:EARLY]
        a_copy(n).start()
        project(n, attended[EARLY:], acc_late, (1 - c) * half)
        return attended

    def project(n, attended, total, first):
        block = 512
        depth = pair_cols(n)

        for k in range(half // block):
            at = slice(k * block, (k + 1) * block)
            column = pl.ds(pl.multiple_of(first + k * block, block), block)
            total[:, at] += jnp.dot(
                attended, w_buf[depth, column], preferred_element_type=jnp.float32
            )

    acc_late[...] = jnp.zeros_like(acc_late)
    acc[...] = jnp.zeros_like(acc)
    def receive(g):
        for side in range(2):
            end = t == (0, times - 1)[side]
            pl.when(has_tm[side])(kv_arrival(side, g).wait_recv)

            @pl.when(end & relayed(g + 1))
            def _():
                kv_arrival(side, g + 1).wait_recv()
                kv_forward(side, g + 1).start()

        kv_local(g).wait()
        q_local(g).wait()

        @pl.when(g + DEPTH < heads)
        def _():
            for side in range(2):
                pl.when(has_height[side])(q_copy(side, g + DEPTH).start)
                pl.when(has_tm[side])(kv_copy(side, g + DEPTH).start)

    def step(n, carry):
        for j in range(PAIR):
            receive(n * PAIR + j)
            attend(n * PAIR + j)

        pl.when(n == 1)(w_copy.wait)

        @pl.when(n > 0)
        def _():
            project(n - 1, combine(n - 1), acc, c * half)

        return carry

    lax.fori_loop(0, pairs, step, 0)

    ahead = pairs // 2
    for n in range(ahead):
        a_copy(n).wait_recv()
    block = 512
    for k in range(half // block):
        column = pl.ds(pl.multiple_of(c * half + k * block, block), block)
        acc_in[:, k * block : (k + 1) * block] = jnp.dot(
            a_in[:, : ahead * width], w_buf[: ahead * width, column],
            preferred_element_type=jnp.float32,
        )
    attended = combine(pairs - 1)
    hid_copy.wait()
    for k in range(CHUNKS):
        piece = slice(k * chunk, (k + 1) * chunk)
        stream = hid_buf[EARLY + k * chunk : EARLY + (k + 1) * chunk, theirs]
        pred_out[piece] = (
            stream.astype(jnp.float32) + gate[:, theirs] * acc_late[piece]
        ).astype(jnp.bfloat16)
        p_copy(k).start()
    project(pairs - 1, attended, acc, c * half)
    for n in range(ahead, pairs):
        a_copy(n).wait_recv()
    for k in range(half // block):
        column = pl.ds(pl.multiple_of(c * half + k * block, block), block)
        acc_in[:, k * block : (k + 1) * block] += jnp.dot(
            a_in[:, ahead * width :], w_buf[ahead * width :, column],
            preferred_element_type=jnp.float32,
        )
    hid_swap.wait_recv()
    gate_swap.wait_recv()

    def guide(k, size, their_pred):
        piece = pl.ds(k * size, size)
        stream = hid_buf[piece, mine].astype(jnp.float32)
        own = (stream + gate[:, mine] * acc[piece]).astype(jnp.bfloat16).astype(jnp.float32)
        cond = jnp.where(c == 0, own, their_pred)
        uncond = jnp.where(c == 0, their_pred, own)
        result[piece] = (uncond + guidance[0] * (cond - uncond)).astype(jnp.bfloat16)

    def store(k):
        piece = pl.ds(k * chunk, chunk)
        return pltpu.make_async_copy(result.at[piece], out.at[0, 0, 0, piece], out_sem.at[k])

    before = EARLY // chunk
    for k in range(before):
        piece = slice(k * chunk, (k + 1) * chunk)
        pred = hid_in[piece].astype(jnp.float32) + gate_in[:, mine] * acc_in[piece]
        guide(k, chunk, pred.astype(jnp.bfloat16).astype(jnp.float32))
        store(k).start()
    for k in range(CHUNKS):
        p_copy(k).wait_recv()
        guide(before + k, chunk, pred_in[k * chunk : (k + 1) * chunk].astype(jnp.float32))
        store(before + k).start()
    for k in range(before + CHUNKS):
        store(k).wait()
    for k in range(CHUNKS):
        p_copy(k).wait_send()
    hid_swap.wait_send()
    gate_swap.wait_send()

    def drain(g, carry):
        for side in range(2):
            end = t == (0, times - 1)[side]
            pl.when(has_tm[side])(kv_copy(side, g).wait_send)
            pl.when(end & relayed(g))(kv_forward(side, g).wait_send)

            @pl.when(has_height[side])
            def _():
                q_copy(side, g).wait_send()
                o_copy(side, g).wait_send()
                l_copy(side, g).wait_send()

        return carry

    lax.fori_loop(0, heads, drain, 0)
    for n in range(pairs):
        a_copy(n).wait_send()


def on_device(query, keyval, hidden, out_weight, gate_scale, guidance, counts):
    rows, channels = query.shape[4], query.shape[5]
    model = hidden.shape[5]
    heads = channels // HEAD_DIM
    bf16, f32, dma = jnp.bfloat16, jnp.float32, pltpu.SemaphoreType.DMA
    anywhere = pl.BlockSpec(memory_space=pl.ANY)
    vmem = pl.BlockSpec(memory_space=pltpu.VMEM)
    smem = pl.BlockSpec(memory_space=pltpu.SMEM)
    return pl.pallas_call(
        kernel,
        out_shape=jax.ShapeDtypeStruct((1, 1, 1, rows, model // 2), bf16),
        in_specs=[anywhere, anywhere, anywhere, anywhere, vmem, smem, smem],
        out_specs=anywhere,
        scratch_shapes=[
            pltpu.VMEM((heads, 3 * rows, HEAD_DIM), bf16),
            pltpu.VMEM((heads, 2, 3 * rows, HEAD_DIM), bf16),
            pltpu.VMEM((channels, model), bf16),
            pltpu.VMEM((rows, model), bf16),
            pltpu.VMEM((heads, rows, HEAD_DIM), f32),
            pltpu.VMEM((2, heads, rows, HEAD_DIM), bf16),
            pltpu.VMEM((2, heads, rows, HEAD_DIM), bf16),
            pltpu.VMEM((heads, rows, HEAD_DIM), f32),
            pltpu.VMEM((2, heads, 8, rows), f32),
            pltpu.VMEM((2, heads, 8, rows), f32),
            pltpu.VMEM((rows, model // 2), f32),
            pltpu.VMEM((rows - EARLY, model // 2), f32),
            pltpu.VMEM((EARLY, model // 2), f32),
            pltpu.VMEM((rows - EARLY, model // 2), bf16),
            pltpu.VMEM((rows - EARLY, model // 2), bf16),
            pltpu.VMEM((EARLY, channels), bf16),
            pltpu.VMEM((EARLY, channels), bf16),
            pltpu.VMEM((EARLY, model // 2), bf16),
            pltpu.VMEM((1, model), f32),
            pltpu.VMEM((rows, model // 2), bf16),
        ]
        + [dma((2, heads))] * 8
        + [dma((heads // PAIR,))] * 2
        + [dma((CHUNKS,))] * 2
        + [dma((2,))] * 2
        + [dma((heads,))] * 2
        + [dma, dma, dma((rows * CHUNKS // (rows - EARLY),))],
        compiler_params=pltpu.CompilerParams(
            collective_id=0, has_side_effects=True, vmem_limit_bytes=60 * 2**20
        ),
    )(query, keyval, hidden, out_weight, gate_scale, guidance, jnp.swapaxes(counts, 1, 2))


def solution(mesh):
    return jax.shard_map(
        on_device,
        mesh=mesh,
        in_specs=(
            P("cfg", "tm", "height", None, None, None),
            P(None, "cfg", "tm", "height", None, None, None),
            P("cfg", "tm", "height", None, None, None),
            P(),
            P("cfg", None),
            P(),
            P(),
        ),
        out_specs=P("tm", "height", None, None, "cfg"),
        check_vma=False,
    )
```

```python
import functools
import math

import jax
import jax.numpy as jnp
from jax import lax
from jax.experimental import pallas as pl
from jax.experimental.pallas import tpu as pltpu
from jax.sharding import PartitionSpec as P

HEAD_DIM = 128
PAIR = 2
DEPTH = 8
EARLY = 256
CHUNKS = 2
MASKED = -1e30
MESH = pl.DeviceIdType.MESH


def kernel(
    query, keyval, hidden, weight, gate, guidance, counts, out,
    q_buf, kv_buf, w_buf, hid_buf, o_own, o_out, o_in, l_own, l_out, l_in,
    acc, acc_late, acc_in, pred_out, pred_in, a_out, a_in, hid_in, gate_in, result,
    kv_send, kv_recv, q_send, q_recv, o_send, o_recv, l_send, l_recv,
    a_send, a_recv, p_send, p_recv, x_send, x_recv, kv_sem, q_sem, w_sem, hid_sem, out_sem,
):
    rows, channels = query.shape[4], query.shape[5]
    heads = channels // HEAD_DIM
    pairs, width = heads // PAIR, PAIR * HEAD_DIM
    model = hidden.shape[5]
    half = model // 2
    scale = HEAD_DIM**-0.5 * math.log2(math.e)

    c, t, h = lax.axis_index("cfg"), lax.axis_index("tm"), lax.axis_index("height")
    times, heights = lax.axis_size("tm"), lax.axis_size("height")
    has_left, has_right = t > 0, t < times - 1
    has_up, has_down = h > 0, h < heights - 1
    left, right, up, down = {"tm": t - 1}, {"tm": t + 1}, {"height": h - 1}, {"height": h + 1}
    other = {"cfg": 1 - c}

    def cols(g):
        return pl.ds(pl.multiple_of(g * HEAD_DIM, HEAD_DIM), HEAD_DIM)

    def pair_cols(n):
        return pl.ds(pl.multiple_of(n * width, width), width)

    def kv_slot(slot, g):
        return kv_buf.at[g, :, pl.ds(pl.multiple_of(slot * rows, rows), rows)]

    def q_slot(slot, g):
        return q_buf.at[g, pl.ds(pl.multiple_of(slot * rows, rows), rows)]

    def kv_local(g):
        return pltpu.make_async_copy(
            keyval.at[:, 0, 0, 0, 0, :, cols(g)], kv_slot(1, g), kv_sem.at[g]
        )

    def q_local(g):
        return pltpu.make_async_copy(
            query.at[0, 0, 0, 0, :, cols(g)], q_slot(1, g), q_sem.at[g]
        )

    middle = times // 2

    def relayed(g):
        return (g >= heads // 6) & (g < heads * 2 // 3)

    def kv_copy(side, g):
        by = relayed(g) & (t == (middle, middle - 1)[side])
        return pltpu.make_async_remote_copy(
            keyval.at[:, 0, 0, 0, 0, :, cols(g)],
            kv_slot(jnp.where(by, 2 * side, 2 - 2 * side), g),
            kv_send.at[side, g],
            kv_recv.at[jnp.where(by, side, 1 - side), g],
            device_id={"tm": jnp.where(by, (0, times - 1)[side], t + (-1, 1)[side])},
            device_id_type=MESH,
        )

    def kv_forward(side, g):
        return pltpu.make_async_remote_copy(
            kv_slot(2 * side, g),
            kv_slot(2 - 2 * side, g),
            kv_send.at[side, g],
            kv_recv.at[1 - side, g],
            device_id={"tm": (middle - 1, middle)[side]},
            device_id_type=MESH,
        )

    def kv_arrival(side, g):
        return pltpu.make_async_remote_copy(
            kv_slot(2 * side, g),
            kv_slot(2 * side, g),
            kv_send.at[side, g],
            kv_recv.at[side, g],
            device_id=other,
            device_id_type=MESH,
        )

    def q_copy(side, g):
        return pltpu.make_async_remote_copy(
            query.at[0, 0, 0, 0, :, cols(g)],
            q_slot(2 - 2 * side, g),
            q_send.at[side, g],
            q_recv.at[1 - side, g],
            device_id=(up, down)[side],
            device_id_type=MESH,
        )

    def o_copy(side, g):
        return pltpu.make_async_remote_copy(
            o_out.at[side, g],
            o_in.at[1 - side, g],
            o_send.at[side, g],
            o_recv.at[1 - side, g],
            device_id=(up, down)[side],
            device_id_type=MESH,
        )

    def l_copy(side, g):
        return pltpu.make_async_remote_copy(
            l_out.at[side, g],
            l_in.at[1 - side, g],
            l_send.at[side, g],
            l_recv.at[1 - side, g],
            device_id=(up, down)[side],
            device_id_type=MESH,
        )

    def a_copy(n):
        return pltpu.make_async_remote_copy(
            a_out.at[:, pair_cols(n)],
            a_in.at[:, pair_cols(n)],
            a_send.at[n],
            a_recv.at[n],
            device_id=other,
            device_id_type=MESH,
        )

    late = rows - EARLY
    chunk = late // CHUNKS

    def p_copy(k):
        piece = pl.ds(k * chunk, chunk)
        return pltpu.make_async_remote_copy(
            pred_out.at[piece],
            pred_in.at[piece],
            p_send.at[k],
            p_recv.at[k],
            device_id=other,
            device_id_type=MESH,
        )

    mine = pl.ds(pl.multiple_of(c * half, half), half)
    theirs = pl.ds(pl.multiple_of((1 - c) * half, half), half)
    hid_swap = pltpu.make_async_remote_copy(
        hidden.at[0, 0, 0, 0, :EARLY, theirs],
        hid_in,
        x_send.at[0],
        x_recv.at[0],
        device_id=other,
        device_id_type=MESH,
    )
    gate_swap = pltpu.make_async_remote_copy(
        gate, gate_in, x_send.at[1], x_recv.at[1], device_id=other, device_id_type=MESH
    )

    has_tm, has_height = (has_left, has_right), (has_up, has_down)

    w_copy = pltpu.make_async_copy(weight, w_buf, w_sem)
    hid_copy = pltpu.make_async_copy(hidden.at[0, 0, 0, 0], hid_buf, hid_sem)
    for g in range(heads):
        kv_local(g).start()
        q_local(g).start()

    barrier = pltpu.get_barrier_semaphore()
    near = jnp.int32(1)
    pl.semaphore_signal(barrier, inc=1, device_id=other, device_id_type=MESH)
    for present, device in (
        (has_left, left), (has_right, right), (has_up, up), (has_down, down)
    ):
        near = near + present.astype(jnp.int32)

        @pl.when(present)
        def _():
            pl.semaphore_signal(barrier, inc=1, device_id=device, device_id_type=MESH)

    for at, far in (
        (0, middle - 1), (0, middle), (middle - 1, 0),
        (middle, 0), (times - 1, middle - 1), (times - 1, middle),
        (middle - 1, times - 1), (middle, times - 1),
    ):
        near = near + (t == at).astype(jnp.int32)

        @pl.when(t == at)
        def _():
            pl.semaphore_signal(barrier, inc=1, device_id={"tm": far}, device_id_type=MESH)

    pl.semaphore_wait(barrier, near)

    for g in range(DEPTH):
        for side in range(2):
            pl.when(has_height[side])(q_copy(side, g).start)
            pl.when(has_tm[side])(kv_copy(side, g).start)
    w_copy.start()
    hid_swap.start()
    gate_swap.start()
    hid_copy.start()

    for side in range(2):

        @pl.when(jnp.logical_not(has_tm[side]))
        def _():
            for g in range(heads):
                if not relayed(g):
                    kv_buf[g, :, 2 * side * rows : (2 * side + 1) * rows] = jnp.zeros(
                        (2, rows, HEAD_DIM), kv_buf.dtype
                    )

        @pl.when(jnp.logical_not(has_height[side]))
        def _():
            q_buf[:, 2 * side * rows : (2 * side + 1) * rows] = jnp.zeros(
                (heads, rows, HEAD_DIM), q_buf.dtype
            )
            o_in[side] = jnp.zeros(o_in.shape[1:], o_in.dtype)
            l_in[side] = jnp.full(l_in.shape[1:], MASKED, l_in.dtype)

    position = lax.broadcasted_iota(jnp.int32, (1, rows), 1)
    live = []
    for step in (-1, 0, 1):
        at = jnp.clip(t + step, 0, times - 1)
        inside = (t + step >= 0) & (t + step < times)
        seen = position < jnp.where(inside, counts[at, 0, h], 0)
        live.append(seen.astype(jnp.int32))
    live = jnp.concatenate(live, axis=1) > 0
    own_count = counts[t, 0, h]
    query_live = (
        lax.broadcasted_iota(jnp.int32, (rows, HEAD_DIM), 0) < own_count
    ).astype(jnp.float32)
    low_lanes = lax.broadcasted_iota(jnp.int32, (rows, HEAD_DIM), 1) < HEAD_DIM // 2
    ones = jnp.ones((3 * rows, HEAD_DIM), jnp.bfloat16)

    def attend_rows(first, size, g):
        scores = lax.dot_general(
            q_buf[g, first : first + size], kv_buf[g, 0], (((1,), (1,)), ((), ())),
            preferred_element_type=jnp.float32,
        )
        scores = jnp.where(live, scores, MASKED)
        top = jnp.max(scores, axis=1, keepdims=True)
        probs = jnp.exp2((scores - top) * scale).astype(jnp.bfloat16)
        values = jnp.concatenate([kv_buf[g, 1], ones], axis=1)
        mixed = jnp.dot(probs, values, preferred_element_type=jnp.float32)
        total = mixed[:, HEAD_DIM:]
        level = top * scale + jnp.log(total) * math.log2(math.e)
        return mixed[:, :HEAD_DIM] / total, level

    def attend(g):
        for side in range(2):
            pl.when(has_height[side])(q_copy(1 - side, g).wait_recv)

        size = 3 * rows // 2
        results = [attend_rows(first, size, g) for first in (0, size)]
        mixed = jnp.concatenate([x for x, _ in results], axis=0)
        level = jnp.concatenate([x for _, x in results], axis=0)
        for side in range(2):
            at = slice(2 * side * rows, (2 * side + 1) * rows)
            o_out[side, g] = mixed[at].astype(jnp.bfloat16)
            l_out[side, g] = jnp.transpose(level[at])[:8]
        o_own[g] = mixed[rows : 2 * rows]
        l_own[g] = level[rows : 2 * rows]
        for side in range(2):

            @pl.when(has_height[side])
            def _():
                o_copy(side, g).start()
                l_copy(side, g).start()

    def combine(n):
        for side in range(2):

            @pl.when(has_height[side])
            def _():
                for j in range(PAIR):
                    o_copy(1 - side, n * PAIR + j).wait_recv()
                    l_copy(1 - side, n * PAIR + j).wait_recv()

        def arrived(side):
            spread = [
                jnp.broadcast_to(l_in[side, n * PAIR + j, :1], (HEAD_DIM // 2, rows))
                for j in range(PAIR)
            ]
            return jnp.transpose(jnp.concatenate(spread, axis=0))

        own_level = jnp.where(low_lanes, l_own[n * PAIR], l_own[n * PAIR + 1])
        levels = [arrived(0), own_level, arrived(1)]
        top = jnp.maximum(jnp.maximum(levels[0], levels[1]), levels[2])
        shares = [jnp.exp2(x - top) for x in levels]
        total = shares[0] + shares[1] + shares[2]
        shares = [x / total * query_live for x in shares]
        parts = []
        for j in range(PAIR):
            lane, g = j * HEAD_DIM // 2, n * PAIR + j
            parts.append(
                shares[0][:, lane : lane + 1] * o_in[0, g].astype(jnp.float32)
                + shares[1][:, lane : lane + 1] * o_own[g]
                + shares[2][:, lane : lane + 1] * o_in[1, g].astype(jnp.float32)
            )
        attended = jnp.concatenate(parts, axis=1).astype(jnp.bfloat16)
        a_out[:, pair_cols(n)] = attended[:EARLY]
        a_copy(n).start()
        project(n, attended[EARLY:], acc_late, (1 - c) * half)
        return attended

    def project(n, attended, total, first):
        block = 512
        depth = pair_cols(n)

        for k in range(half // block):
            at = slice(k * block, (k + 1) * block)
            column = pl.ds(pl.multiple_of(first + k * block, block), block)
            total[:, at] += jnp.dot(
                attended, w_buf[depth, column], preferred_element_type=jnp.float32
            )

    acc_late[...] = jnp.zeros_like(acc_late)
    acc[...] = jnp.zeros_like(acc)
    def receive(g):
        for side in range(2):
            end = t == (0, times - 1)[side]
            pl.when(has_tm[side])(kv_arrival(side, g).wait_recv)

            @pl.when(end & relayed(g + 1))
            def _():
                kv_arrival(side, g + 1).wait_recv()
                kv_forward(side, g + 1).start()

        kv_local(g).wait()
        q_local(g).wait()

        @pl.when(g + DEPTH < heads)
        def _():
            for side in range(2):
                pl.when(has_height[side])(q_copy(side, g + DEPTH).start)
                pl.when(has_tm[side])(kv_copy(side, g + DEPTH).start)

    def step(n, carry):
        receive(n * PAIR)
        attend(n * PAIR)
        pl.when(n == 1)(w_copy.wait)

        @pl.when(n > 0)
        def _():
            project(n - 1, combine(n - 1), acc, c * half)

        for j in range(1, PAIR):
            receive(n * PAIR + j)
            attend(n * PAIR + j)

        return carry

    lax.fori_loop(0, pairs, step, 0)

    ahead = pairs // 2
    for n in range(ahead):
        a_copy(n).wait_recv()
    block = 512
    for k in range(half // block):
        column = pl.ds(pl.multiple_of(c * half + k * block, block), block)
        acc_in[:, k * block : (k + 1) * block] = jnp.dot(
            a_in[:, : ahead * width], w_buf[: ahead * width, column],
            preferred_element_type=jnp.float32,
        )
    attended = combine(pairs - 1)
    hid_copy.wait()
    for k in range(CHUNKS):
        piece = slice(k * chunk, (k + 1) * chunk)
        stream = hid_buf[EARLY + k * chunk : EARLY + (k + 1) * chunk, theirs]
        pred_out[piece] = (
            stream.astype(jnp.float32) + gate[:, theirs] * acc_late[piece]
        ).astype(jnp.bfloat16)
        p_copy(k).start()
    project(pairs - 1, attended, acc, c * half)
    for n in range(ahead, pairs):
        a_copy(n).wait_recv()
    for k in range(half // block):
        column = pl.ds(pl.multiple_of(c * half + k * block, block), block)
        acc_in[:, k * block : (k + 1) * block] += jnp.dot(
            a_in[:, ahead * width :], w_buf[ahead * width :, column],
            preferred_element_type=jnp.float32,
        )
    hid_swap.wait_recv()
    gate_swap.wait_recv()

    def guide(k, size, their_pred):
        piece = pl.ds(k * size, size)
        stream = hid_buf[piece, mine].astype(jnp.float32)
        own = (stream + gate[:, mine] * acc[piece]).astype(jnp.bfloat16).astype(jnp.float32)
        cond = jnp.where(c == 0, own, their_pred)
        uncond = jnp.where(c == 0, their_pred, own)
        result[piece] = (uncond + guidance[0] * (cond - uncond)).astype(jnp.bfloat16)

    def store(k):
        piece = pl.ds(k * chunk, chunk)
        return pltpu.make_async_copy(result.at[piece], out.at[0, 0, 0, piece], out_sem.at[k])

    before = EARLY // chunk
    for k in range(before):
        piece = slice(k * chunk, (k + 1) * chunk)
        pred = hid_in[piece].astype(jnp.float32) + gate_in[:, mine] * acc_in[piece]
        guide(k, chunk, pred.astype(jnp.bfloat16).astype(jnp.float32))
        store(k).start()
    for k in range(CHUNKS):
        p_copy(k).wait_recv()
        guide(before + k, chunk, pred_in[k * chunk : (k + 1) * chunk].astype(jnp.float32))
        store(before + k).start()
    for k in range(before + CHUNKS):
        store(k).wait()
    for k in range(CHUNKS):
        p_copy(k).wait_send()
    hid_swap.wait_send()
    gate_swap.wait_send()

    def drain(g, carry):
        for side in range(2):
            end = t == (0, times - 1)[side]
            pl.when(has_tm[side])(kv_copy(side, g).wait_send)
            pl.when(end & relayed(g))(kv_forward(side, g).wait_send)

            @pl.when(has_height[side])
            def _():
                q_copy(side, g).wait_send()
                o_copy(side, g).wait_send()
                l_copy(side, g).wait_send()

        return carry

    lax.fori_loop(0, heads, drain, 0)
    for n in range(pairs):
        a_copy(n).wait_send()


def on_device(query, keyval, hidden, out_weight, gate_scale, guidance, counts):
    rows, channels = query.shape[4], query.shape[5]
    model = hidden.shape[5]
    heads = channels // HEAD_DIM
    bf16, f32, dma = jnp.bfloat16, jnp.float32, pltpu.SemaphoreType.DMA
    anywhere = pl.BlockSpec(memory_space=pl.ANY)
    vmem = pl.BlockSpec(memory_space=pltpu.VMEM)
    smem = pl.BlockSpec(memory_space=pltpu.SMEM)
    return pl.pallas_call(
        kernel,
        out_shape=jax.ShapeDtypeStruct((1, 1, 1, rows, model // 2), bf16),
        in_specs=[anywhere, anywhere, anywhere, anywhere, vmem, smem, smem],
        out_specs=anywhere,
        scratch_shapes=[
            pltpu.VMEM((heads, 3 * rows, HEAD_DIM), bf16),
            pltpu.VMEM((heads, 2, 3 * rows, HEAD_DIM), bf16),
            pltpu.VMEM((channels, model), bf16),
            pltpu.VMEM((rows, model), bf16),
            pltpu.VMEM((heads, rows, HEAD_DIM), f32),
            pltpu.VMEM((2, heads, rows, HEAD_DIM), bf16),
            pltpu.VMEM((2, heads, rows, HEAD_DIM), bf16),
            pltpu.VMEM((heads, rows, HEAD_DIM), f32),
            pltpu.VMEM((2, heads, 8, rows), f32),
            pltpu.VMEM((2, heads, 8, rows), f32),
            pltpu.VMEM((rows, model // 2), f32),
            pltpu.VMEM((rows - EARLY, model // 2), f32),
            pltpu.VMEM((EARLY, model // 2), f32),
            pltpu.VMEM((rows - EARLY, model // 2), bf16),
            pltpu.VMEM((rows - EARLY, model // 2), bf16),
            pltpu.VMEM((EARLY, channels), bf16),
            pltpu.VMEM((EARLY, channels), bf16),
            pltpu.VMEM((EARLY, model // 2), bf16),
            pltpu.VMEM((1, model), f32),
            pltpu.VMEM((rows, model // 2), bf16),
        ]
        + [dma((2, heads))] * 8
        + [dma((heads // PAIR,))] * 2
        + [dma((CHUNKS,))] * 2
        + [dma((2,))] * 2
        + [dma((heads,))] * 2
        + [dma, dma, dma((rows * CHUNKS // (rows - EARLY),))],
        compiler_params=pltpu.CompilerParams(
            collective_id=0, has_side_effects=True, vmem_limit_bytes=60 * 2**20
        ),
    )(query, keyval, hidden, out_weight, gate_scale, guidance, jnp.swapaxes(counts, 1, 2))


def solution(mesh):
    return jax.shard_map(
        on_device,
        mesh=mesh,
        in_specs=(
            P("cfg", "tm", "height", None, None, None),
            P(None, "cfg", "tm", "height", None, None, None),
            P("cfg", "tm", "height", None, None, None),
            P(),
            P("cfg", None),
            P(),
            P(),
        ),
        out_specs=P("tm", "height", None, None, "cfg"),
        check_vma=False,
    )
```
